32 devices in a mesh: sect: 2 (over y), batch: 8 (over z, core), head: 2 (over x).
Axes of the slice: x: 2, y: 2, z: 4, core: 2. Of those that a mesh axis runs over, the one named last changes fastest.
Arguments:
- queries: bfloat16 [48, 16, 512], P('batch', 'head', 'sect'), may hold values from -51 to 51
- newest_key_value: bfloat16 [48, 4, 256], P('batch'), may hold values from -5 to 5
- page_cache: bfloat16 [48, 256, 64, 256], P('batch', ('sect', 'head')), may hold values from -4 to 4
- lengths: int32 [48], P('batch'), may hold values from 2048 to 4096, as said below
- page_ids: int32 [48, 4, 32], P('batch'), may hold values from 0 to 63, as said below
- out_weight: bfloat16 [8192, 4096], P(('sect', 'head'), 'batch'), may hold values from -0.0625 to 0.0625
- residual: bfloat16 [48, 4096], P(None, 'batch'), may hold values from -2 to 2
- norm_gain: float32 [4096], P('batch'), may hold values from 0.25 to 1.75
- expert_ids: int32 [48, 8], replicated, may hold values from 0 to 63, all different within a row; in each aligned block of 48 rows (0 to 47, 48 to 95, ...) at most 12 rows name the same one
- route_weight: float32 [48, 8], replicated, may hold values from 0.1 to 1
- gate_up_weight: bfloat16 [32, 4096, 2, 3072], P(('sect', 'batch'), None, None, 'head'), may hold values from -0.09375 to 0.09375
- down_weight: bfloat16 [32, 3072, 4096], P(('sect', 'batch'), 'head'), may hold values from -0.15625 to 0.15625
Outputs:
- layer_out: bfloat16 [48, 4096], P(None, 'batch')
The draws below stay inside these ranges and needn't reach their ends.
Inputs may be any that keep to these rules, and one draw needn't show every extreme that they name: `lengths`: some sequence holds exactly 4096 cached tokens and some exactly 2048. `page_ids`: each row lists 32 different pages in ascending order, all below the number of pages that hold the sequence's cached tokens, and always the last of those pages. `expert_ids`: each row names 8 different experts; over all rows no expert is named by more than 12 rows, a bound that some block reaches.
All inputs are finite; a program needn't handle non-finite values.
Results may differ from the reference program's by a relative error of at most 0.025.
Values may be sent and summed in bfloat16 or wider, within the bound.
A program may use at most 192 MiB of HBM per device.

```python
import math
import jax
import jax.numpy as jnp
import numpy as np
from jax import lax

D = 4096
QUERY_HEADS = 64
KEY_VALUE_HEADS = 4
HEAD_WIDTH = 128
FFE = 1536
EXPERTS = 64
TOPK = 8
PAGE_TOKENS = 64
PAGES_READ = 32
SEQUENCE_PAGES = 64
SEQUENCE_COUNT = 48
CAP = 12


def draw_plan(key):
    base_key = jax.random.fold_in(key, 7001)
    length_key, page_score_key = jax.random.split(base_key)
    lengths = jax.random.randint(length_key, (SEQUENCE_COUNT,), PAGES_READ * PAGE_TOKENS, SEQUENCE_PAGES * PAGE_TOKENS + 1, dtype=jnp.int32)
    lengths = lengths.at[0].set(SEQUENCE_PAGES * PAGE_TOKENS).at[1].set(PAGES_READ * PAGE_TOKENS)
    valid_pages = (lengths + PAGE_TOKENS - 1) // PAGE_TOKENS
    random_jitter = jax.random.randint(page_score_key, (SEQUENCE_COUNT, KEY_VALUE_HEADS, SEQUENCE_PAGES), 0, 65536, dtype=jnp.int32)
    page_index = jnp.arange(SEQUENCE_PAGES, dtype=jnp.int32)
    ranking = (random_jitter + page_index * 1024) * SEQUENCE_PAGES + page_index
    last_page = valid_pages[:, None, None] - 1
    ranking = jnp.where(page_index == last_page, 2 ** 30, ranking)
    ranking = jnp.where(page_index > last_page, -1, ranking)
    unused, picked = lax.top_k(ranking, PAGES_READ)
    return (lengths.astype(jnp.int32), jnp.sort(picked, axis=-1).astype(jnp.int32))


def cache_base(key):
    cache_key = jax.random.fold_in(key, 7002)
    cache_layout = (SEQUENCE_COUNT, KEY_VALUE_HEADS * SEQUENCE_PAGES, PAGE_TOKENS, 2 * HEAD_WIDTH)
    cache_values = jnp.clip(jax.random.normal(cache_key, cache_layout, jnp.float32), -4.0, 4.0)
    return cache_values


def draw_lengths(key, part):
    return draw_plan(key)[0]


def draw_page_ids(key, part):
    return draw_plan(key)[1]


def draw_page_cache(key, part):
    return cache_base(key).astype(jnp.bfloat16)


def draw_queries(key, part):
    query_key = jax.random.fold_in(key, 7003)
    values = jnp.clip(3.0 * jax.random.normal(query_key, (SEQUENCE_COUNT, QUERY_HEADS, HEAD_WIDTH), jnp.float32), -12.0, 12.0)
    values = values.reshape(SEQUENCE_COUNT, KEY_VALUE_HEADS, QUERY_HEADS // KEY_VALUE_HEADS, HEAD_WIDTH).transpose(0, 2, 1, 3)
    return values.reshape(SEQUENCE_COUNT, QUERY_HEADS // KEY_VALUE_HEADS, KEY_VALUE_HEADS * HEAD_WIDTH).astype(jnp.bfloat16)


def block_scale(stream_key, shape, cuts, smallest, top_value):
    gain, own = 1.0, jax.random.fold_in(stream_key, 6)
    for axis_at, shards_of in cuts:
        draws = jnp.exp(jax.random.uniform(jax.random.fold_in(own, axis_at), (shards_of,), jnp.float32, smallest / len(cuts), top_value / len(cuts)))
        gain = gain * jnp.repeat(draws, shape[axis_at] // shards_of).reshape([-1 if axis == axis_at else 1 for axis in range(len(shape))])
    return gain


def assign_block(rng, own, number, rows, number_of, top, limit, skew):
    sequence = jax.random.permutation(rng, number_of)
    heavy_load, common = shares(number_of, rows * top, limit, skew, True), shares(number_of, rows * top, limit, skew, False)
    places = jnp.arange(number_of)

    def named(sizes, offset_by):
        used = int((sizes > 0).sum())
        fixed = max(1, used // 4)
        passed = fixed + (places - fixed + offset_by * (used - fixed)) % max(1, number_of - fixed)
        return jnp.zeros((number_of,), jnp.int32).at[sequence[jnp.where(places < fixed, places, passed)]].set(jnp.asarray(sizes, jnp.int32))

    sizes = jnp.where(number % 4 == 0, named(heavy_load, number // 4), named(common, number - number // 4 - 1))
    mixed = jax.random.permutation(jax.random.fold_in(own, 3), number_of)
    donor, taker = mixed[0:number_of // 2 * 2:2], mixed[1:number_of // 2 * 2:2]
    margin = jnp.minimum(sizes[donor] - 1, limit - sizes[taker]) // 2
    margin = jnp.where((donor == sequence[0]) | (taker == sequence[0]) | (sizes[taker] == 0), 0, jnp.maximum(margin, 0))
    passed = jax.random.randint(jax.random.fold_in(own, 4), (number_of // 2,), 0, 1 << 20) % (margin + 1)
    sizes = sizes.at[donor].add(-passed).at[taker].add(passed)
    labels = jnp.searchsorted(jnp.cumsum(sizes), jnp.arange(rows * top), side="right").astype(jnp.int32)
    grid = labels.reshape(top, rows).T
    grid = grid[jax.random.permutation(jax.random.fold_in(own, 1), rows)]
    offset_by = jax.random.randint(jax.random.fold_in(own, 2), (rows, 1), 0, top)
    return jnp.take_along_axis(grid, (jnp.arange(top)[None, :] + offset_by) % top, axis=1)


def shares(amount, total, limit, skew, full):
    weights = [(1 << 20) // math.isqrt(rank ** skew) + 1 for rank in range(1, amount + 1)]
    largest = limit if full else min(limit, max(-(-total // amount), total * weights[0] // sum(weights)))
    least = 1 if total - largest >= amount - 1 else 0
    holding, spare = [largest] + [least] * (amount - 1), total - largest - least * (amount - 1)
    while spare > 0:
        candidates = [i for i in range(1, amount) if holding[i] < largest] or [i for i in range(1, amount) if holding[i] < limit]
        mass, remaining = sum([weights[i] for i in candidates]), spare
        for i in candidates:
            extra = min(limit - holding[i], max(1, remaining * weights[i] // mass), spare)
            holding[i] = holding[i] + extra
            spare = spare - extra
    return np.array(holding)


def noise(own_key, extent, deviation, most, cuts=(), kind=jnp.bfloat16):
    result = jax.random.normal(own_key, extent, jnp.float32) * deviation
    if len(cuts) > 0:
        result = block_scale(own_key, extent, cuts, -0.22, 0.18) * result
    return jnp.clip(result, min=-most, max=most).astype(kind)


def setup_inputs(seed: int = 0) -> dict:
    splits = jax.random.split(jax.random.key(seed), 13)
    queries = draw_queries(jax.random.fold_in(splits[12], 71), 0)
    newest_key_value = noise(splits[1], (SEQUENCE_COUNT, KEY_VALUE_HEADS, 2 * HEAD_WIDTH), 1.0, 5.0, ((0, 8),))
    page_cache = draw_page_cache(jax.random.fold_in(splits[12], 71), 0)
    lengths = draw_lengths(jax.random.fold_in(splits[12], 71), 0)
    page_ids = draw_page_ids(jax.random.fold_in(splits[12], 71), 0)
    out_weight = noise(splits[5], (QUERY_HEADS * HEAD_WIDTH, D), (QUERY_HEADS * HEAD_WIDTH) ** -0.5, 0.0625, ((0, 4), (1, 8)))
    residual = noise(splits[6], (SEQUENCE_COUNT, D), 0.3, 2.0, ((1, 8),))
    norm_gain = jnp.clip(1.0 + 0.15 * jax.random.normal(splits[7], (D,), jnp.float32), 0.25, 1.75)
    expert_ids_keys = jax.random.split(jax.random.fold_in(splits[8], 1), SEQUENCE_COUNT // SEQUENCE_COUNT)
    expert_ids_turns = jax.random.permutation(jax.random.fold_in(splits[8], 3), SEQUENCE_COUNT // SEQUENCE_COUNT)
    expert_ids = jax.vmap(lambda own, number: assign_block(jax.random.fold_in(splits[8], 2), own, number, SEQUENCE_COUNT, EXPERTS, TOPK, CAP, 2))(expert_ids_keys, expert_ids_turns).reshape((SEQUENCE_COUNT, TOPK))
    route_weight = jnp.clip(jax.random.uniform(splits[9], (SEQUENCE_COUNT, TOPK), jnp.float32, 0.1, 1.0), 0.1, 1.0)
    gate_up_weight = noise(splits[10], (EXPERTS // 2, D, 2, 2 * FFE), D ** -0.5, 0.09375, ((0, 16), (3, 2)))
    down_weight = noise(splits[11], (EXPERTS // 2, 2 * FFE, D), FFE ** -0.5, 0.15625, ((0, 16), (1, 2)))
    return {"queries": queries, "newest_key_value": newest_key_value, "page_cache": page_cache, "lengths": lengths, "page_ids": page_ids, "out_weight": out_weight, "residual": residual, "norm_gain": norm_gain, "expert_ids": expert_ids, "route_weight": route_weight, "gate_up_weight": gate_up_weight, "down_weight": down_weight}


NEG_FILL = -1e+30
NORM_EPS = 1e-06

def attend_one(entries):
    single_query, newest_entry, cache_entries, sequence_length, chosen = entries
    heads_in_group = QUERY_HEADS // KEY_VALUE_HEADS
    scaling = 1.0 / math.sqrt(HEAD_WIDTH)
    query_groups = single_query.reshape(heads_in_group, KEY_VALUE_HEADS, HEAD_WIDTH).transpose(1, 0, 2).astype(jnp.float32)
    cache_entries = cache_entries.reshape(KEY_VALUE_HEADS, SEQUENCE_PAGES, PAGE_TOKENS, 2 * HEAD_WIDTH)
    block_list = jax.vmap(lambda stored, picked: stored[picked])(cache_entries, chosen)
    token_place = chosen[:, :, None] * PAGE_TOKENS + jnp.arange(PAGE_TOKENS, dtype=jnp.int32)[None, None, :]
    usable_pages = (token_place < sequence_length).reshape(KEY_VALUE_HEADS, PAGES_READ * PAGE_TOKENS)
    usable_pages = jnp.concatenate([usable_pages, jnp.ones((KEY_VALUE_HEADS, 1), dtype=jnp.bool_)], axis=1)
    gathered_keys = jnp.concatenate([block_list[..., :HEAD_WIDTH].reshape(KEY_VALUE_HEADS, PAGES_READ * PAGE_TOKENS, HEAD_WIDTH), newest_entry[:, None, :HEAD_WIDTH]], axis=1).astype(jnp.float32)
    gathered_values = jnp.concatenate([block_list[..., HEAD_WIDTH:].reshape(KEY_VALUE_HEADS, PAGES_READ * PAGE_TOKENS, HEAD_WIDTH), newest_entry[:, None, HEAD_WIDTH:]], axis=1).astype(jnp.float32)
    scores = jnp.einsum('ghd,gkd->ghk', query_groups, gathered_keys) * scaling
    scores = jnp.where(usable_pages[:, None, :], scores, NEG_FILL)
    row_peak = lax.optimization_barrier(jnp.max(scores, axis=2, keepdims=True))
    weights = jnp.where(usable_pages[:, None, :], jnp.exp(scores - row_peak), 0.0)
    totals = lax.optimization_barrier(jnp.sum(weights, axis=2))
    rounded = weights.astype(jnp.bfloat16).astype(jnp.float32)
    mixture = jnp.einsum('ghk,gkd->ghd', rounded, gathered_values) / totals[..., None]
    return mixture.reshape(QUERY_HEADS * HEAD_WIDTH).astype(jnp.bfloat16)

def expert_one(inputs, gate_up, down_part):
    mixture = jnp.dot(inputs, gate_up.reshape(D, 2 * FFE), preferred_element_type=jnp.float32)
    activated = (jax.nn.silu(mixture[:, :FFE]) * mixture[:, FFE:]).astype(jnp.bfloat16)
    return jnp.dot(activated, down_part, preferred_element_type=jnp.float32)

def pair_pass(entries):
    inputs, gate_up, down_part = entries
    first = expert_one(inputs[0], gate_up[:, :, :FFE], down_part[:FFE])
    second = expert_one(inputs[1], gate_up[:, :, FFE:], down_part[FFE:])
    return jnp.stack([first, second])

def reference(queries, newest_key_value, page_cache, lengths, page_ids, out_weight, residual, norm_gain, expert_ids, route_weight, gate_up_weight, down_weight):
    attention = lax.map(attend_one, (queries, newest_key_value, page_cache, lengths, page_ids))
    projected = jnp.dot(attention, out_weight, preferred_element_type=jnp.float32)
    hidden_state = residual.astype(jnp.float32) + projected
    inverse = lax.rsqrt(lax.optimization_barrier(jnp.mean(hidden_state * hidden_state, axis=1)) + NORM_EPS)
    normed = (hidden_state * inverse[:, None] * norm_gain[None, :]).astype(jnp.bfloat16)
    flat_ids = expert_ids.reshape(-1)
    one_hot = (flat_ids[:, None] == jnp.arange(EXPERTS, dtype=jnp.int32)[None, :]).astype(jnp.int32)
    rank_in = lax.optimization_barrier(jnp.sum((jnp.cumsum(one_hot, axis=0) - one_hot) * one_hot, axis=1))
    slot_index = (flat_ids * CAP + rank_in).astype(jnp.int32)
    token_index = jnp.repeat(jnp.arange(SEQUENCE_COUNT, dtype=jnp.int32), TOPK)
    dispatched = jnp.zeros((EXPERTS * CAP, D), jnp.bfloat16).at[slot_index].set(normed[token_index])
    dispatched = dispatched.reshape(EXPERTS // 2, 2, CAP, D)
    outputs = lax.map(pair_pass, (dispatched, gate_up_weight, down_weight)).reshape(EXPERTS * CAP, D)
    gathered = outputs[slot_index].reshape(SEQUENCE_COUNT, TOPK, D)
    coefficient = route_weight / lax.optimization_barrier(jnp.sum(route_weight, axis=1, keepdims=True))
    expert_mix = lax.optimization_barrier(jnp.sum(coefficient[:, :, None] * gathered, axis=1))
    return (hidden_state + expert_mix).astype(jnp.bfloat16)
```

```python
import functools
import math

import jax
import jax.numpy as jnp
from jax import lax
from jax.experimental import pallas as pl
from jax.experimental.pallas import tpu as pltpu
from jax.sharding import PartitionSpec as P

D = 4096
EXPERTS = 64


MESH = pl.DeviceIdType.MESH
NEG_FILL = -1e30
NORM_EPS = 1e-06


def as_sent(shard):
    return jax.tree.map(lambda a: a.astype(jnp.bfloat16) if a.dtype == jnp.float32 else a, shard)


def from_partner(shard, axis, distance):
    return lax.ppermute(shard, axis, [(i, i ^ 1 << distance) for i in range(lax.axis_size(axis))])


def merge_pair(first, second):
    first_max, first_sum, first_acc = first
    second_max, second_sum, second_acc = second
    joined = jnp.maximum(first_max, second_max)
    first_factor = jnp.exp(first_max - joined)
    second_factor = jnp.exp(second_max - joined)
    return (
        joined,
        first_sum * first_factor + second_sum * second_factor,
        first_acc * first_factor[..., None] + second_acc * second_factor[..., None],
    )


def head_slice(partial_value, begin_at, span_size):
    return tuple(
        (lax.dynamic_slice_in_dim(member, begin_at, span_size, 1) for member in partial_value)
    )


def on_device(
    queries,
    newest_key_value,
    page_cache,
    lengths,
    page_ids,
    out_weight,
    residual,
    norm_gain,
    expert_ids,
    route_weight,
    gate_up_weight,
    down_weight,
):
    seq_count = queries.shape[0]
    head_dim = newest_key_value.shape[2] // 2
    kv_heads = newest_key_value.shape[1]
    sect_size = lax.axis_size("sect")
    head_size = lax.axis_size("head")
    batch_size = lax.axis_size("batch")
    group_size = sect_size * head_size // kv_heads
    position = lax.axis_index("sect") * head_size + lax.axis_index("head")
    kv_index = position // group_size
    quarter = position % group_size
    local_pages = page_cache.shape[1]
    page_len = page_cache.shape[2]
    scaling = 1.0 / math.sqrt(head_dim)
    all_heads = lax.all_gather(queries, "head", axis=1, tiled=True)
    kv_local = kv_index % (kv_heads // sect_size)
    group_query = lax.dynamic_slice_in_dim(all_heads, kv_local * head_dim, head_dim, 2)
    heads_dev = all_heads.shape[1] // group_size
    block_cols = heads_dev * head_dim
    chosen = lax.dynamic_index_in_dim(page_ids, kv_index, 1, keepdims=False)
    leading_page = quarter * local_pages
    page_number = jnp.broadcast_to(
        leading_page + jnp.arange(local_pages, dtype=jnp.int32), (seq_count, local_pages)
    )
    page_used = jnp.any(chosen[:, :, None] == page_number[:, None, :], axis=1)
    token_place = (
        page_number[:, :, None] * page_len + jnp.arange(page_len, dtype=jnp.int32)[None, None, :]
    )
    key_count = page_cache.shape[1] * page_len
    usable_pages = (page_used[:, :, None] & (token_place < lengths[:, None, None])).reshape(
        seq_count, key_count
    )
    gathered_keys = page_cache[..., :head_dim].reshape(seq_count, key_count, head_dim)
    gathered_values = page_cache[..., head_dim:].reshape(seq_count, key_count, head_dim)
    scores = (
        jnp.einsum("shd,skd->shk", group_query, gathered_keys, preferred_element_type=jnp.float32)
        * scaling
    )
    scores = jnp.where(usable_pages[:, None, :], scores, NEG_FILL)
    newest_entry = lax.dynamic_index_in_dim(newest_key_value, kv_index, 1, keepdims=False)
    fresh_score = (
        jnp.einsum(
            "shd,sd->sh",
            group_query,
            newest_entry[:, :head_dim],
            preferred_element_type=jnp.float32,
        )
        * scaling
    )
    leading = quarter == 0
    fresh_score = jnp.where(leading, fresh_score, NEG_FILL)
    running_max = jnp.maximum(jnp.max(scores, axis=2), fresh_score)
    weights = jnp.where(usable_pages[:, None, :], jnp.exp(scores - running_max[..., None]), 0.0)
    fresh_weight = jnp.where(leading, jnp.exp(fresh_score - running_max), 0.0)
    running_sum = jnp.sum(weights, axis=2) + fresh_weight
    weighted = jnp.einsum(
        "shk,skd->shd",
        weights.astype(jnp.bfloat16),
        gathered_values,
        preferred_element_type=jnp.float32,
    )
    weighted = weighted + fresh_weight.astype(jnp.bfloat16).astype(jnp.float32)[
        ..., None
    ] * newest_entry[:, None, head_dim:].astype(jnp.float32)
    partial_value = (running_max, running_sum, weighted)
    bit_count = group_size.bit_length() - 1
    for bit_index in range(bit_count):
        partner = from_partner(
            (as_sent(partial_value[0]), as_sent(partial_value[1]), as_sent(partial_value[2])),
            "head",
            bit_index,
        )
        partial_value = merge_pair(partial_value, partner)
    partial_value = head_slice(partial_value, quarter * heads_dev, heads_dev)
    attention = (
        (partial_value[2] / partial_value[1][..., None])
        .reshape(seq_count, block_cols)
        .astype(jnp.bfloat16)
    )
    head_terms = jnp.dot(
        lax.all_gather(attention, "batch", axis=0, tiled=True),
        out_weight,
        preferred_element_type=jnp.float32,
    )
    projected = lax.psum(head_terms.astype(jnp.bfloat16), ("sect", "head")).astype(jnp.float32)
    hidden_state = residual.astype(jnp.float32) + projected
    squares = lax.psum(jnp.sum(hidden_state * hidden_state, axis=1), "batch")
    inverse = lax.rsqrt(squares / D + NORM_EPS)
    normed = (hidden_state * inverse[:, None] * norm_gain[None, :]).astype(jnp.bfloat16)
    token_count, top_count = expert_ids.shape
    capacity = 2 * token_count * top_count // EXPERTS
    pair_local = gate_up_weight.shape[0]
    flat_ids = expert_ids.reshape(-1)
    one_hot = (flat_ids[:, None] == jnp.arange(EXPERTS, dtype=jnp.int32)[None, :]).astype(jnp.int32)
    earlier = jnp.cumsum(one_hot, axis=0) - one_hot
    rank_in = jnp.sum(earlier * one_hot, axis=1)
    sub_half = lax.axis_index("head") // (head_size // 2)
    pair_first = lax.axis_index("sect") * (batch_size * pair_local)
    local_pair = flat_ids // 2 - pair_first
    in_sect = (local_pair >= 0) & (local_pair < batch_size * pair_local)
    full_slot = (
        (local_pair // pair_local * 2 + flat_ids % 2) * pair_local + local_pair % pair_local
    ) * capacity + rank_in
    full_slot = jnp.where(in_sect, full_slot, -1)
    slot_dev = pair_local * capacity
    slot_total = batch_size * 2 * slot_dev
    send_count = batch_size * slot_dev
    matches = (
        full_slot.reshape(token_count, top_count)[None, :, :]
        == jnp.arange(slot_total, dtype=jnp.int32)[:, None, None]
    )
    selector_full = (
        jnp.any(matches, axis=2).astype(jnp.bfloat16).reshape(batch_size, 2, slot_dev, token_count)
    )
    selector = lax.dynamic_index_in_dim(selector_full, sub_half, 1, keepdims=False).reshape(
        send_count, token_count
    )
    coefficient = route_weight / jnp.sum(route_weight, axis=1, keepdims=True)
    combine_full = jnp.sum(jnp.where(matches, coefficient[None, :, :], 0.0), axis=2).T
    cols_dev = normed.shape[1]
    outgoing = jnp.dot(selector, normed, preferred_element_type=jnp.float32).astype(jnp.bfloat16)
    outgoing = outgoing.reshape(batch_size, pair_local, capacity, cols_dev)
    arrived = lax.all_to_all(outgoing, "batch", split_axis=0, concat_axis=3, tiled=True)[0]
    mixture = jnp.einsum(
        "ecd,edgf->ecgf", arrived, gate_up_weight, preferred_element_type=jnp.float32
    )
    activated = (jax.nn.silu(mixture[:, :, 0]) * mixture[:, :, 1]).astype(jnp.bfloat16)
    expert_part = jnp.einsum(
        "ecf,efd->ecd", activated, down_weight, preferred_element_type=jnp.float32
    )
    leaving = expert_part.reshape(1, slot_dev, batch_size, cols_dev)
    came_back = (
        lax.all_to_all(
            leaving.astype(jnp.bfloat16), "batch", split_axis=2, concat_axis=0, tiled=True
        )
        .astype(leaving.dtype)
        .reshape(send_count, cols_dev)
    )
    weights_used = lax.dynamic_index_in_dim(
        combine_full.reshape(token_count, batch_size, 2, slot_dev), sub_half, 2, keepdims=False
    )
    weights_used = weights_used.reshape(token_count, send_count)
    combined = jnp.dot(
        weights_used, came_back, precision=lax.Precision.HIGHEST, preferred_element_type=jnp.float32
    )
    expert_mix = lax.psum(combined.astype(jnp.bfloat16), ("sect", "head")).astype(jnp.float32)
    return (hidden_state + expert_mix).astype(jnp.bfloat16)


NG = 12


def layer_kernel(
    dims,
    queries_ref, newest_ref, lengths_ref, pages_ref, residual_ref, gain_ref, ids_ref, route_ref,
    cache_hbm, ow_hbm, gate_hbm, down_hbm,
    out_ref,
    cbuf, owbuf, gbuf, dbuf,
    used_ref, q_out, q_in, attn_all, attn_f32, lhs, psum_buf, hidden_ref, sq_all,
    sel_ref, sel16, whi_ref, wlo_ref, disp_out, disp_in, x2, acc, act_ref, res_ref,
    ret_out, ret_in, cb_ref, fin_buf,
    c_sem, ow_sem, g_sem, d_sem, q_sem, at_s, at_r, p_s, p_r, s_s, s_r, x_s, x_r, r_s, r_r, f_s, f_r,
):
    S, B, H, R, CAPN, CH, DC = dims
    f32, bf16 = jnp.float32, jnp.bfloat16
    seqs, pages, plen, _ = cbuf.shape
    hd = cbuf.shape[3] // 2
    keys = pages * plen
    tokens, cols = residual_ref.shape
    group = S * H
    pairs = gate_hbm.shape[0]
    depth = gate_hbm.shape[1]
    ff = gate_hbm.shape[3]
    nchunk = depth // CH
    ndown = ff // DC
    half = cols // 2
    scaling = 1.0 / math.sqrt(hd)
    sect, b, h = lax.axis_index("sect"), lax.axis_index("batch"), lax.axis_index("head")
    pos = sect * H + h

    def cache_copy(i):
        return pltpu.make_async_copy(cache_hbm.at[i], cbuf.at[i], c_sem.at[i])

    def gate_copy(c):
        slot = c % NG
        return pltpu.make_async_copy(
            gate_hbm.at[c // nchunk, pl.ds((c % nchunk) * CH, CH)], gbuf.at[slot], g_sem.at[slot]
        )

    def down_copy(c):
        return pltpu.make_async_copy(
            down_hbm.at[c // ndown, pl.ds((c % ndown) * DC, DC)], dbuf.at[c], d_sem.at[c]
        )

    ow_copy = pltpu.make_async_copy(ow_hbm, owbuf, ow_sem)
    for i in range(seqs):
        cache_copy(i).start()
    ow_copy.start()

    barrier = pltpu.get_barrier_semaphore()

    def batch_peer(k):
        return (sect, lax.rem(b + k, B), h)

    def group_peer(k):
        p = lax.rem(pos + k, group)
        return (p // H, b, p % H)

    for k in range(1, B):
        pl.semaphore_signal(barrier, inc=1, device_id=batch_peer(k), device_id_type=MESH)
    for k in range(1, group):
        pl.semaphore_signal(barrier, inc=1, device_id=group_peer(k), device_id_type=MESH)

    q_all = queries_ref[...].astype(f32)
    q_first, q_second = q_all[:, :, :hd], q_all[:, :, hd:]
    q_in[h] = jnp.where(h == 0, q_first, q_second)
    q_out[...] = jnp.where(h == 0, q_second, q_first)

    pl.semaphore_wait(barrier, B - 1 + group - 1)

    q_copy = pltpu.make_async_remote_copy(
        src_ref=q_out, dst_ref=q_in.at[h], send_sem=q_sem.at[0], recv_sem=q_sem.at[1],
        device_id=(sect, b, 1 - h), device_id_type=MESH,
    )
    q_copy.start()

    chosen = jnp.zeros((seqs, pages_ref.shape[2]), jnp.int32)
    for k in range(pages_ref.shape[1]):
        chosen = chosen + jnp.where(pos == k, pages_ref[:, k, :], 0)
    page_iota = lax.broadcasted_iota(jnp.int32, (seqs, pages), 1)
    used = jnp.zeros((seqs, pages), f32)
    for j in range(pages_ref.shape[2]):
        used = jnp.maximum(used, jnp.where(chosen[:, j : j + 1] == page_iota, 1.0, 0.0))
    spread_low = lax.broadcasted_iota(jnp.int32, (pages, keys), 0) * plen
    spread_at = lax.broadcasted_iota(jnp.int32, (pages, keys), 1)
    spread = jnp.where((spread_at >= spread_low) & (spread_at < spread_low + plen), 1.0, 0.0)
    used_ref[0:seqs, :] = jnp.dot(used.astype(bf16), spread.astype(bf16), preferred_element_type=f32)

    count = B * pairs
    slots = count * CAPN
    expert = 2 * (sect * count + lax.broadcasted_iota(jnp.int32, (count, tokens), 0)) + h
    route = route_ref[...]
    coef = route / jnp.sum(route, axis=0, keepdims=True)
    member = jnp.zeros((count, tokens), f32)
    amount = jnp.zeros((count, tokens), f32)
    for k in range(ids_ref.shape[0]):
        hit = ids_ref[k : k + 1, :] == expert
        member = jnp.where(hit, 1.0, member)
        amount = jnp.where(hit, coef[k : k + 1, :], amount)
    before = jnp.where(
        lax.broadcasted_iota(jnp.int32, (tokens, tokens), 0)
        < lax.broadcasted_iota(jnp.int32, (tokens, tokens), 1), 1.0, 0.0
    )
    rank = jnp.dot(member.astype(bf16), before.astype(bf16), preferred_element_type=f32)
    rank = jnp.where(member > 0.5, rank, -1.0)
    slot_row = lax.broadcasted_iota(jnp.int32, (slots, count), 0)
    slot_low = lax.broadcasted_iota(jnp.int32, (slots, count), 1) * CAPN
    widen = jnp.where((slot_row >= slot_low) & (slot_row < slot_low + CAPN), 1.0, 0.0)
    within = jnp.sum(widen * (slot_row - slot_low).astype(f32), axis=1, keepdims=True)
    widen = widen.astype(bf16)
    slot_rank = jnp.dot(widen, rank.astype(bf16), preferred_element_type=f32)
    sel = jnp.where(slot_rank == within, 1.0, 0.0)
    sel_ref[...] = sel
    sel16[...] = sel.astype(bf16)
    amount_hi = amount.astype(bf16)
    amount_lo = (amount - amount_hi.astype(f32)).astype(bf16)
    eye = jnp.where(
        lax.broadcasted_iota(jnp.int32, (tokens, tokens), 0)
        == lax.broadcasted_iota(jnp.int32, (tokens, tokens), 1), 1.0, 0.0
    ).astype(bf16)
    for part, target in ((amount_hi, whi_ref), (amount_lo, wlo_ref)):
        rows = (sel * jnp.dot(widen, part, preferred_element_type=f32)).astype(bf16)
        target[...] = lax.dot_general(
            eye, rows, (((1,), (1,)), ((), ())), preferred_element_type=f32
        ).astype(bf16)

    q_copy.wait()

    per_seq = NG // seqs

    @pl.loop(0, seqs)
    def _(i):
        cache_copy(i).wait()
        for n in range(per_seq):
            gate_copy(i * per_seq + n).start()
        q = jnp.concatenate([q_in[0, i], q_in[1, i]], axis=0)
        k_mat = cbuf[i, :, :, 0:hd].reshape(keys, hd)
        scores = lax.dot_general(
            q.astype(bf16), k_mat, (((1,), (1,)), ((), ())), preferred_element_type=f32
        ) * scaling
        at = lax.broadcasted_iota(jnp.int32, (1, keys), 1)
        usable = (used_ref[pl.ds(i, 1), :] > 0.5) & (at < lengths_ref[i])
        fill = jnp.where(usable, 0.0, 1.0)
        scores = jnp.where(fill > 0.5, NEG_FILL, scores)
        fresh = newest_ref[i].astype(f32)
        mine = lax.broadcasted_iota(jnp.int32, fresh.shape, 0) == pos
        fresh = jnp.sum(jnp.where(mine, fresh, 0.0), axis=0, keepdims=True)
        fresh_score = jnp.sum(q * fresh[:, :hd], axis=1, keepdims=True) * scaling
        top = jnp.maximum(jnp.max(scores, axis=1, keepdims=True), fresh_score)
        weights = jnp.where(fill > 0.5, 0.0, jnp.exp(scores - top))
        fresh_weight = jnp.exp(fresh_score - top)
        total = jnp.sum(weights, axis=1, keepdims=True) + fresh_weight
        v_mat = cbuf[i, :, :, hd : 2 * hd].reshape(keys, hd)
        mixed = jnp.dot(weights.astype(bf16), v_mat, preferred_element_type=f32)
        mixed = mixed + fresh_weight.astype(bf16).astype(f32) * fresh[:, hd:]
        attn_all[b, i] = (mixed / total).astype(bf16)

    def to_batch(src_at, dst, send_sem, recv_sem):
        copies = []
        for k in range(1, B):
            peer = batch_peer(k)
            copies.append(
                pltpu.make_async_remote_copy(
                    src_ref=src_at(peer[1]), dst_ref=dst.at[b],
                    send_sem=send_sem.at[k - 1], recv_sem=recv_sem.at[k - 1],
                    device_id=peer, device_id_type=MESH,
                )
            )
        for copy in copies:
            copy.start()
        return copies

    def to_group(buf, send_sem, recv_sem):
        copies = []
        for k in range(1, group):
            copies.append(
                pltpu.make_async_remote_copy(
                    src_ref=buf.at[pos], dst_ref=buf.at[pos],
                    send_sem=send_sem.at[k - 1], recv_sem=recv_sem.at[k - 1],
                    device_id=group_peer(k), device_id_type=MESH,
                )
            )
        for copy in copies:
            copy.start()
        return copies

    def finish(copies):
        for copy in copies:
            copy.wait()

    gather = to_batch(lambda peer: attn_all.at[b], attn_all, at_s, at_r)

    @pl.loop(0, pairs * ndown)
    def _(c):
        down_copy(c).start()

    finish(gather)

    heads = attn_all.shape[2]
    attn_f32[...] = attn_all[...].reshape(tokens, heads, hd).astype(f32)
    for j in range(heads):
        lhs[:, j * hd : (j + 1) * hd] = attn_f32[:, j, :].astype(bf16)
    ow_copy.wait()
    psum_buf[pos] = jnp.dot(lhs[...], owbuf[...], preferred_element_type=f32).astype(bf16)
    finish(to_group(psum_buf, p_s, p_r))
    projected = psum_buf[0].astype(f32)
    for p in range(1, group):
        projected = projected + psum_buf[p].astype(f32)
    hidden = residual_ref[...].astype(f32) + projected
    hidden_ref[...] = hidden

    gained = (hidden * gain_ref[...].reshape(1, cols)).astype(bf16)
    picked = jnp.dot(sel16[...], gained, preferred_element_type=f32)
    for t in range(B):
        piece = picked[t * R : (t + 1) * R]
        disp_out[t] = jnp.concatenate([piece[:, :half], piece[:, half:]], axis=0).astype(bf16)
    dispatch = to_batch(lambda peer: disp_out.at[peer], disp_in, x_s, x_r)
    squares = jnp.sum(hidden * hidden, axis=1, keepdims=True)
    diag = lax.broadcasted_iota(jnp.int32, (tokens, 128), 0) == lax.broadcasted_iota(
        jnp.int32, (tokens, 128), 1
    )
    sq_row = jnp.sum(jnp.where(diag, squares, 0.0), axis=0, keepdims=True)
    sq_all[b] = jnp.broadcast_to(sq_row, (8, 128))
    sq_copies = to_batch(lambda peer: sq_all.at[b], sq_all, s_s, s_r)
    disp_in[b] = disp_out[b]
    z_row = 2 * lax.broadcasted_iota(jnp.int32, (128, 512), 0)
    z_col = lax.broadcasted_iota(jnp.int32, (128, 512), 1)
    place = jnp.where((z_col == z_row) | (z_col == z_row + 257), 1.0, 0.0).astype(bf16)
    finish(dispatch)

    @pl.loop(0, B)
    def _(s):
        got = disp_in[s].astype(f32)
        pieces = []
        for n in range(cols // 128):
            top_row = 0 if n * 128 < half else R
            at = n * 128 % half
            pieces.append(got[top_row : top_row + R, at : at + 128])
        spread_x = jnp.dot(
            jnp.concatenate(pieces, axis=0).astype(bf16), place, preferred_element_type=f32
        )
        for n in range(cols // 128):
            rows = spread_x[n * R : (n + 1) * R]
            to = pl.multiple_of(s * (2 * cols) + n * 256, 256)
            x2[:, pl.ds(to, 256)] = jnp.concatenate(
                [rows[:, :256], rows[:, 256:]], axis=0
            ).astype(bf16)

    finish(sq_copies)
    sq_total = sq_all[0]
    for t in range(1, B):
        sq_total = sq_total + sq_all[t]
    inverse = lax.rsqrt(sq_total / D + NORM_EPS)[0:1, 0:tokens]
    own = sel_ref[pl.ds(pl.multiple_of(b * R, 8), R), :]
    row_inverse = jnp.sum(own * inverse, axis=1, keepdims=True)
    row_number = lax.broadcasted_iota(jnp.int32, (R, ff), 0)

    res_ref[...] = jnp.zeros_like(res_ref)
    for e in range(pairs):
        acc[...] = jnp.zeros_like(acc)

        @pl.loop(0, nchunk)
        def _(c):
            at = e * nchunk + c
            gate_copy(at).wait()
            weight = gbuf.at[at % NG].reshape(2 * CH, ff)
            left = x2[:, pl.ds(pl.multiple_of(c * (2 * CH), 2 * CH), 2 * CH)]
            acc[...] += jnp.dot(left, weight[...], preferred_element_type=f32)

            @pl.when(at + NG < pairs * nchunk)
            def _():
                gate_copy(at + NG).start()

        gate = acc[0:R] * row_inverse
        up = acc[R : 2 * R] * row_inverse
        value = gate * (1.0 / (1.0 + jnp.exp(-gate))) * up
        held = (row_number >= e * CAPN) & (row_number < (e + 1) * CAPN)
        act_ref[...] = jnp.where(held, value, 0.0).astype(bf16)

        @pl.loop(0, ndown)
        def _(c):
            at = e * ndown + c
            down_copy(at).wait()
            left = act_ref[:, pl.ds(pl.multiple_of(c * DC, DC), DC)]
            res_ref[...] += jnp.dot(left, dbuf[at], preferred_element_type=f32)

    for t in range(B):
        piece = res_ref[:, t * cols : (t + 1) * cols]
        ret_out[t] = jnp.concatenate([piece[:, :half], piece[:, half:]], axis=0).astype(bf16)
    back = to_batch(lambda peer: ret_out.at[peer], ret_in, r_s, r_r)
    ret_in[b] = ret_out[b]
    finish(back)
    for t in range(B):
        piece = ret_in[t].astype(f32)
        cb_ref[t * R : (t + 1) * R, :half] = piece[:R]
        cb_ref[t * R : (t + 1) * R, half:] = piece[R:]
    came = cb_ref[...].astype(bf16)
    combined = jnp.dot(whi_ref[...], came, preferred_element_type=f32) + jnp.dot(
        wlo_ref[...], came, preferred_element_type=f32
    )
    fin_buf[pos] = combined.astype(bf16)
    finish(to_group(fin_buf, f_s, f_r))
    mix = fin_buf[0].astype(f32)
    for p in range(1, group):
        mix = mix + fin_buf[p].astype(f32)
    out_ref[...] = (hidden_ref[...] + mix).astype(out_ref.dtype)


def fused(
    queries, newest, cache, lengths, page_ids, out_weight, residual, gain, ids, route, gate_up, down
):
    S, B, H = lax.axis_size("sect"), lax.axis_size("batch"), lax.axis_size("head")
    seqs, qh, _ = queries.shape
    hd = newest.shape[2] // 2
    tokens, cols = residual.shape
    pairs, depth, _, ff = gate_up.shape
    capn = 2 * tokens * ids.shape[1] // EXPERTS
    R = pairs * capn
    CH, DC = 256, 256
    keys = cache.shape[1] * cache.shape[2]
    slots = B * R
    group = S * H
    bf16, f32 = jnp.bfloat16, jnp.float32
    V, dma = pltpu.VMEM, pltpu.SemaphoreType.DMA
    vm, hbm = pl.BlockSpec(memory_space=pltpu.VMEM), pl.BlockSpec(memory_space=pl.ANY)
    smem = pl.BlockSpec(memory_space=pltpu.SMEM)
    ndown = ff // DC
    return pl.pallas_call(
        functools.partial(layer_kernel, (S, B, H, R, capn, CH, DC)),
        out_shape=jax.ShapeDtypeStruct((tokens, cols), bf16),
        in_specs=[vm, vm, smem, vm, vm, vm, vm, vm, hbm, hbm, hbm, hbm],
        out_specs=vm,
        scratch_shapes=[
            V(cache.shape, bf16), V(out_weight.shape, bf16), V((NG, CH, 2, ff), bf16),
            V((pairs * ndown, DC, depth), bf16),
            V((-(-seqs // 8) * 8, keys), f32), V((seqs, qh, hd), f32), V((H, seqs, qh, hd), f32),
            V((B, seqs, qh * H, hd), bf16), V((tokens, qh * H, hd), f32),
            V((tokens, qh * H * hd), bf16), V((group, tokens, cols), bf16), V((tokens, cols), f32),
            V((B, 8, 128), f32),
            V((slots, tokens), f32), V((slots, tokens), bf16), V((tokens, slots), bf16),
            V((tokens, slots), bf16), V((B, 2 * R, cols // 2), bf16),
            V((B, 2 * R, cols // 2), bf16), V((2 * R, 2 * depth), bf16), V((2 * R, ff), f32),
            V((R, ff), bf16), V((R, depth), f32),
            V((B, 2 * R, cols // 2), bf16), V((B, 2 * R, cols // 2), bf16), V((slots, cols), f32),
            V((group, tokens, cols), bf16),
            dma((seqs,)), dma, dma((NG,)), dma((pairs * ndown,)), dma((2,)),
            dma((B - 1,)), dma((B - 1,)), dma((group - 1,)), dma((group - 1,)),
            dma((B - 1,)), dma((B - 1,)), dma((B - 1,)), dma((B - 1,)),
            dma((B - 1,)), dma((B - 1,)), dma((group - 1,)), dma((group - 1,)),
        ],
        compiler_params=pltpu.CompilerParams(
            collective_id=0, has_side_effects=True, vmem_limit_bytes=63 * 1024 * 1024
        ),
        cost_estimate=pl.CostEstimate(
            flops=4 * R * depth * ff * pairs * 3,
            bytes_accessed=2 * (gate_up.size + down.size + cache.size), transcendentals=0,
        ),
    )(queries, newest, lengths, page_ids, residual, gain, ids.T, route.T,
      cache, out_weight, gate_up, down)


def solution(mesh):
    placed = (
        P("batch", "head", "sect"),
        P("batch", None, None),
        P("batch", ("sect", "head"), None, None),
        P("batch"),
        P("batch", None, None),
        P(("sect", "head"), "batch"),
        P(None, "batch"),
        P("batch"),
        P(),
        P(),
        P(("sect", "batch"), None, None, "head"),
        P(("sect", "batch"), "head", None),
    )
    whole_parts = mesh.shape["sect"] * mesh.shape["head"] == 4 and mesh.shape["head"] == 2
    body = fused if whole_parts else on_device
    return jax.shard_map(
        body, mesh=mesh, in_specs=placed, out_specs=P(None, "batch"), check_vma=False
    )
```

```python
import functools
import math

import jax
import jax.numpy as jnp
from jax import lax
from jax.experimental import pallas as pl
from jax.experimental.pallas import tpu as pltpu
from jax.sharding import PartitionSpec as P

D = 4096
EXPERTS = 64


MESH = pl.DeviceIdType.MESH
NEG_FILL = -1e30
NORM_EPS = 1e-06


def as_sent(shard):
    return jax.tree.map(lambda a: a.astype(jnp.bfloat16) if a.dtype == jnp.float32 else a, shard)


def from_partner(shard, axis, distance):
    return lax.ppermute(shard, axis, [(i, i ^ 1 << distance) for i in range(lax.axis_size(axis))])


def merge_pair(first, second):
    first_max, first_sum, first_acc = first
    second_max, second_sum, second_acc = second
    joined = jnp.maximum(first_max, second_max)
    first_factor = jnp.exp(first_max - joined)
    second_factor = jnp.exp(second_max - joined)
    return (
        joined,
        first_sum * first_factor + second_sum * second_factor,
        first_acc * first_factor[..., None] + second_acc * second_factor[..., None],
    )


def head_slice(partial_value, begin_at, span_size):
    return tuple(
        (lax.dynamic_slice_in_dim(member, begin_at, span_size, 1) for member in partial_value)
    )


def on_device(
    queries,
    newest_key_value,
    page_cache,
    lengths,
    page_ids,
    out_weight,
    residual,
    norm_gain,
    expert_ids,
    route_weight,
    gate_up_weight,
    down_weight,
):
    seq_count = queries.shape[0]
    head_dim = newest_key_value.shape[2] // 2
    kv_heads = newest_key_value.shape[1]
    sect_size = lax.axis_size("sect")
    head_size = lax.axis_size("head")
    batch_size = lax.axis_size("batch")
    group_size = sect_size * head_size // kv_heads
    position = lax.axis_index("sect") * head_size + lax.axis_index("head")
    kv_index = position // group_size
    quarter = position % group_size
    local_pages = page_cache.shape[1]
    page_len = page_cache.shape[2]
    scaling = 1.0 / math.sqrt(head_dim)
    all_heads = lax.all_gather(queries, "head", axis=1, tiled=True)
    kv_local = kv_index % (kv_heads // sect_size)
    group_query = lax.dynamic_slice_in_dim(all_heads, kv_local * head_dim, head_dim, 2)
    heads_dev = all_heads.shape[1] // group_size
    block_cols = heads_dev * head_dim
    chosen = lax.dynamic_index_in_dim(page_ids, kv_index, 1, keepdims=False)
    leading_page = quarter * local_pages
    page_number = jnp.broadcast_to(
        leading_page + jnp.arange(local_pages, dtype=jnp.int32), (seq_count, local_pages)
    )
    page_used = jnp.any(chosen[:, :, None] == page_number[:, None, :], axis=1)
    token_place = (
        page_number[:, :, None] * page_len + jnp.arange(page_len, dtype=jnp.int32)[None, None, :]
    )
    key_count = page_cache.shape[1] * page_len
    usable_pages = (page_used[:, :, None] & (token_place < lengths[:, None, None])).reshape(
        seq_count, key_count
    )
    gathered_keys = page_cache[..., :head_dim].reshape(seq_count, key_count, head_dim)
    gathered_values = page_cache[..., head_dim:].reshape(seq_count, key_count, head_dim)
    scores = (
        jnp.einsum("shd,skd->shk", group_query, gathered_keys, preferred_element_type=jnp.float32)
        * scaling
    )
    scores = jnp.where(usable_pages[:, None, :], scores, NEG_FILL)
    newest_entry = lax.dynamic_index_in_dim(newest_key_value, kv_index, 1, keepdims=False)
    fresh_score = (
        jnp.einsum(
            "shd,sd->sh",
            group_query,
            newest_entry[:, :head_dim],
            preferred_element_type=jnp.float32,
        )
        * scaling
    )
    leading = quarter == 0
    fresh_score = jnp.where(leading, fresh_score, NEG_FILL)
    running_max = jnp.maximum(jnp.max(scores, axis=2), fresh_score)
    weights = jnp.where(usable_pages[:, None, :], jnp.exp(scores - running_max[..., None]), 0.0)
    fresh_weight = jnp.where(leading, jnp.exp(fresh_score - running_max), 0.0)
    running_sum = jnp.sum(weights, axis=2) + fresh_weight
    weighted = jnp.einsum(
        "shk,skd->shd",
        weights.astype(jnp.bfloat16),
        gathered_values,
        preferred_element_type=jnp.float32,
    )
    weighted = weighted + fresh_weight.astype(jnp.bfloat16).astype(jnp.float32)[
        ..., None
    ] * newest_entry[:, None, head_dim:].astype(jnp.float32)
    partial_value = (running_max, running_sum, weighted)
    bit_count = group_size.bit_length() - 1
    for bit_index in range(bit_count):
        partner = from_partner(
            (as_sent(partial_value[0]), as_sent(partial_value[1]), as_sent(partial_value[2])),
            "head",
            bit_index,
        )
        partial_value = merge_pair(partial_value, partner)
    partial_value = head_slice(partial_value, quarter * heads_dev, heads_dev)
    attention = (
        (partial_value[2] / partial_value[1][..., None])
        .reshape(seq_count, block_cols)
        .astype(jnp.bfloat16)
    )
    head_terms = jnp.dot(
        lax.all_gather(attention, "batch", axis=0, tiled=True),
        out_weight,
        preferred_element_type=jnp.float32,
    )
    projected = lax.psum(head_terms.astype(jnp.bfloat16), ("sect", "head")).astype(jnp.float32)
    hidden_state = residual.astype(jnp.float32) + projected
    squares = lax.psum(jnp.sum(hidden_state * hidden_state, axis=1), "batch")
    inverse = lax.rsqrt(squares / D + NORM_EPS)
    normed = (hidden_state * inverse[:, None] * norm_gain[None, :]).astype(jnp.bfloat16)
    token_count, top_count = expert_ids.shape
    capacity = 2 * token_count * top_count // EXPERTS
    pair_local = gate_up_weight.shape[0]
    flat_ids = expert_ids.reshape(-1)
    one_hot = (flat_ids[:, None] == jnp.arange(EXPERTS, dtype=jnp.int32)[None, :]).astype(jnp.int32)
    earlier = jnp.cumsum(one_hot, axis=0) - one_hot
    rank_in = jnp.sum(earlier * one_hot, axis=1)
    sub_half = lax.axis_index("head") // (head_size // 2)
    pair_first = lax.axis_index("sect") * (batch_size * pair_local)
    local_pair = flat_ids // 2 - pair_first
    in_sect = (local_pair >= 0) & (local_pair < batch_size * pair_local)
    full_slot = (
        (local_pair // pair_local * 2 + flat_ids % 2) * pair_local + local_pair % pair_local
    ) * capacity + rank_in
    full_slot = jnp.where(in_sect, full_slot, -1)
    slot_dev = pair_local * capacity
    slot_total = batch_size * 2 * slot_dev
    send_count = batch_size * slot_dev
    matches = (
        full_slot.reshape(token_count, top_count)[None, :, :]
        == jnp.arange(slot_total, dtype=jnp.int32)[:, None, None]
    )
    selector_full = (
        jnp.any(matches, axis=2).astype(jnp.bfloat16).reshape(batch_size, 2, slot_dev, token_count)
    )
    selector = lax.dynamic_index_in_dim(selector_full, sub_half, 1, keepdims=False).reshape(
        send_count, token_count
    )
    coefficient = route_weight / jnp.sum(route_weight, axis=1, keepdims=True)
    combine_full = jnp.sum(jnp.where(matches, coefficient[None, :, :], 0.0), axis=2).T
    cols_dev = normed.shape[1]
    outgoing = jnp.dot(selector, normed, preferred_element_type=jnp.float32).astype(jnp.bfloat16)
    outgoing = outgoing.reshape(batch_size, pair_local, capacity, cols_dev)
    arrived = lax.all_to_all(outgoing, "batch", split_axis=0, concat_axis=3, tiled=True)[0]
    mixture = jnp.einsum(
        "ecd,edgf->ecgf", arrived, gate_up_weight, preferred_element_type=jnp.float32
    )
    activated = (jax.nn.silu(mixture[:, :, 0]) * mixture[:, :, 1]).astype(jnp.bfloat16)
    expert_part = jnp.einsum(
        "ecf,efd->ecd", activated, down_weight, preferred_element_type=jnp.float32
    )
    leaving = expert_part.reshape(1, slot_dev, batch_size, cols_dev)
    came_back = (
        lax.all_to_all(
            leaving.astype(jnp.bfloat16), "batch", split_axis=2, concat_axis=0, tiled=True
        )
        .astype(leaving.dtype)
        .reshape(send_count, cols_dev)
    )
    weights_used = lax.dynamic_index_in_dim(
        combine_full.reshape(token_count, batch_size, 2, slot_dev), sub_half, 2, keepdims=False
    )
    weights_used = weights_used.reshape(token_count, send_count)
    combined = jnp.dot(
        weights_used, came_back, precision=lax.Precision.HIGHEST, preferred_element_type=jnp.float32
    )
    expert_mix = lax.psum(combined.astype(jnp.bfloat16), ("sect", "head")).astype(jnp.float32)
    return (hidden_state + expert_mix).astype(jnp.bfloat16)


NG = 7
CACHE_SLOTS = 3
BACK_ROWS = 16


def layer_kernel(
    dims,
    queries_ref, newest_ref, lengths_ref, pages_ref, residual_ref, gain_ref, ids_ref, route_ref,
    cache_hbm, ow_hbm, gate_hbm, down_hbm,
    out_ref,
    cbuf, owbuf, gbuf, dbuf,
    used_ref, q_out, q_in, attn_all, attn_f32, lhs, psum_buf, hidden_ref, sq_all,
    sel_ref, sel16, whi_ref, wlo_ref, disp_out, disp_in, x2, acc, act_ref, res_ref,
    ret_out, ret_in, cb_ref, fin_buf,
    c_sem, ow_sem, g_sem, d_sem, q_sem, at_s, at_r, p_s, p_r, s_s, s_r, x_s, x_r, r_s, r_r, f_s, f_r,
):
    S, B, H, R, CAPN, CH, DC = dims
    f32, bf16 = jnp.float32, jnp.bfloat16
    seqs, pages, plen, _ = cache_hbm.shape
    hd = cbuf.shape[3] // 2
    slots_c = cbuf.shape[0]
    keys = pages * plen
    tokens, cols = residual_ref.shape
    group = S * H
    pairs = gate_hbm.shape[0]
    depth = gate_hbm.shape[1]
    ff = gate_hbm.shape[3]
    nchunk = depth // CH
    ndown = ff // DC
    half = cols // 2
    scaling = 1.0 / math.sqrt(hd)
    sect, b, h = lax.axis_index("sect"), lax.axis_index("batch"), lax.axis_index("head")
    pos = sect * H + h

    def cache_copy(i):
        return pltpu.make_async_copy(cache_hbm.at[i], cbuf.at[i % slots_c], c_sem.at[i % slots_c])

    def gate_copy(c):
        slot = c % NG
        return pltpu.make_async_copy(
            gate_hbm.at[c // nchunk, pl.ds((c % nchunk) * CH, CH)], gbuf.at[slot, :, :, pl.ds(0, ff)],
            g_sem.at[slot],
        )

    def down_copy(c):
        return pltpu.make_async_copy(
            down_hbm.at[c // ndown, pl.ds((c % ndown) * DC, DC)], dbuf.at[c], d_sem.at[c]
        )

    ow_copy = pltpu.make_async_copy(ow_hbm, owbuf, ow_sem)
    for i in range(slots_c):
        cache_copy(i).start()
    ow_copy.start()

    barrier = pltpu.get_barrier_semaphore()

    def batch_peer(k):
        return (sect, lax.rem(b + k, B), h)

    def group_peer(k):
        p = lax.rem(pos + k, group)
        return (p // H, b, p % H)

    for k in range(1, B):
        pl.semaphore_signal(barrier, inc=1, device_id=batch_peer(k), device_id_type=MESH)
    for k in range(1, group):
        pl.semaphore_signal(barrier, inc=1, device_id=group_peer(k), device_id_type=MESH)

    q_all = queries_ref[...].astype(f32)
    q_first, q_second = q_all[:, :, :hd], q_all[:, :, hd:]
    q_in[h] = jnp.where(h == 0, q_first, q_second)
    q_out[...] = jnp.where(h == 0, q_second, q_first)

    pl.semaphore_wait(barrier, B - 1 + group - 1)

    q_copy = pltpu.make_async_remote_copy(
        src_ref=q_out, dst_ref=q_in.at[h], send_sem=q_sem.at[0], recv_sem=q_sem.at[1],
        device_id=(sect, b, 1 - h), device_id_type=MESH,
    )
    q_copy.start()

    chosen = jnp.zeros((seqs, pages_ref.shape[2]), jnp.int32)
    for k in range(pages_ref.shape[1]):
        chosen = chosen + jnp.where(pos == k, pages_ref[:, k, :], 0)
    page_iota = lax.broadcasted_iota(jnp.int32, (seqs, pages), 1)
    used = jnp.zeros((seqs, pages), f32)
    for j in range(pages_ref.shape[2]):
        used = jnp.maximum(used, jnp.where(chosen[:, j : j + 1] == page_iota, 1.0, 0.0))
    spread_low = lax.broadcasted_iota(jnp.int32, (pages, keys), 0) * plen
    spread_at = lax.broadcasted_iota(jnp.int32, (pages, keys), 1)
    spread = jnp.where((spread_at >= spread_low) & (spread_at < spread_low + plen), 1.0, 0.0)
    used_ref[0:seqs, :] = jnp.dot(used.astype(bf16), spread.astype(bf16), preferred_element_type=f32)

    count = B * pairs
    slots = count * CAPN
    expert = 2 * (sect * count + lax.broadcasted_iota(jnp.int32, (count, tokens), 0)) + h
    route = route_ref[...]
    coef = route / jnp.sum(route, axis=0, keepdims=True)
    member = jnp.zeros((count, tokens), f32)
    amount = jnp.zeros((count, tokens), f32)
    for k in range(ids_ref.shape[0]):
        hit = ids_ref[k : k + 1, :] == expert
        member = jnp.where(hit, 1.0, member)
        amount = jnp.where(hit, coef[k : k + 1, :], amount)
    before = jnp.where(
        lax.broadcasted_iota(jnp.int32, (tokens, tokens), 0)
        < lax.broadcasted_iota(jnp.int32, (tokens, tokens), 1), 1.0, 0.0
    )
    rank = jnp.dot(member.astype(bf16), before.astype(bf16), preferred_element_type=f32)
    rank = jnp.where(member > 0.5, rank, -1.0)
    slot_row = lax.broadcasted_iota(jnp.int32, (slots, count), 0)
    slot_low = lax.broadcasted_iota(jnp.int32, (slots, count), 1) * CAPN
    widen = jnp.where((slot_row >= slot_low) & (slot_row < slot_low + CAPN), 1.0, 0.0)
    within = jnp.sum(widen * (slot_row - slot_low).astype(f32), axis=1, keepdims=True)
    widen = widen.astype(bf16)
    slot_rank = jnp.dot(widen, rank.astype(bf16), preferred_element_type=f32)
    sel = jnp.where(slot_rank == within, 1.0, 0.0)
    sel_ref[...] = sel
    sel16[...] = sel.astype(bf16)
    amount_hi = amount.astype(bf16)
    amount_lo = (amount - amount_hi.astype(f32)).astype(bf16)
    eye = jnp.where(
        lax.broadcasted_iota(jnp.int32, (tokens, tokens), 0)
        == lax.broadcasted_iota(jnp.int32, (tokens, tokens), 1), 1.0, 0.0
    ).astype(bf16)
    for part, target in ((amount_hi, whi_ref), (amount_lo, wlo_ref)):
        rows = (sel * jnp.dot(widen, part, preferred_element_type=f32)).astype(bf16)
        target[...] = lax.dot_general(
            eye, rows, (((1,), (1,)), ((), ())), preferred_element_type=f32
        ).astype(bf16)

    q_copy.wait()

    def attend(i):
        cache_copy(i).wait()
        held = cbuf.at[i % slots_c]
        q = jnp.concatenate([q_in[0, i], q_in[1, i]], axis=0)
        k_mat = held[:, :, 0:hd].reshape(keys, hd)
        scores = lax.dot_general(
            q.astype(bf16), k_mat, (((1,), (1,)), ((), ())), preferred_element_type=f32
        ) * scaling
        at = lax.broadcasted_iota(jnp.int32, (1, keys), 1)
        usable = (used_ref[pl.ds(i, 1), :] > 0.5) & (at < lengths_ref[i])
        fill = jnp.where(usable, 0.0, 1.0)
        scores = jnp.where(fill > 0.5, NEG_FILL, scores)
        fresh = newest_ref[i].astype(f32)
        mine = lax.broadcasted_iota(jnp.int32, fresh.shape, 0) == pos
        fresh = jnp.sum(jnp.where(mine, fresh, 0.0), axis=0, keepdims=True)
        fresh_score = jnp.sum(q * fresh[:, :hd], axis=1, keepdims=True) * scaling
        top = jnp.maximum(jnp.max(scores, axis=1, keepdims=True), fresh_score)
        weights = jnp.where(fill > 0.5, 0.0, jnp.exp(scores - top))
        fresh_weight = jnp.exp(fresh_score - top)
        total = jnp.sum(weights, axis=1, keepdims=True) + fresh_weight
        v_mat = held[:, :, hd : 2 * hd].reshape(keys, hd)
        mixed = jnp.dot(weights.astype(bf16), v_mat, preferred_element_type=f32)
        mixed = mixed + fresh_weight.astype(bf16).astype(f32) * fresh[:, hd:]
        attn_all[b, i] = (mixed / total).astype(bf16)

        @pl.when(i + slots_c < seqs)
        def _():
            cache_copy(i + slots_c).start()

    def to_batch(src_at, dst_at, send_sem, recv_sem, first=0):
        copies = []
        for k in range(1, B):
            peer = batch_peer(k)
            copies.append(
                pltpu.make_async_remote_copy(
                    src_ref=src_at(peer[1]), dst_ref=dst_at,
                    send_sem=send_sem.at[first + k - 1], recv_sem=recv_sem.at[first + k - 1],
                    device_id=peer, device_id_type=MESH,
                )
            )
        for copy in copies:
            copy.start()
        return copies

    def to_group(buf, send_sem, recv_sem):
        copies = []
        for k in range(1, group):
            copies.append(
                pltpu.make_async_remote_copy(
                    src_ref=buf.at[pos], dst_ref=buf.at[pos],
                    send_sem=send_sem.at[k - 1], recv_sem=recv_sem.at[k - 1],
                    device_id=group_peer(k), device_id_type=MESH,
                )
            )
        for copy in copies:
            copy.start()
        return copies

    def finish(copies):
        for copy in copies:
            copy.wait()

    part = seqs // 2

    @pl.loop(0, part)
    def _(i):
        attend(i)

    early = attn_all.at[b, pl.ds(0, part)]
    gather = to_batch(lambda peer: early, early, at_s, at_r)
    for c in range(NG):
        gate_copy(c).start()

    @pl.loop(part, seqs)
    def _(i):
        attend(i)

    late = attn_all.at[b, pl.ds(part, seqs - part)]
    gather = gather + to_batch(lambda peer: late, late, at_s, at_r, B - 1)

    @pl.loop(0, pairs * ndown)
    def _(c):
        down_copy(c).start()

    finish(gather)

    heads = attn_all.shape[2]
    attn_f32[...] = attn_all[...].reshape(tokens, heads, hd).astype(f32)
    for j in range(heads):
        lhs[:, j * hd : (j + 1) * hd] = attn_f32[:, j, :].astype(bf16)
    ow_copy.wait()
    psum_buf[pos] = jnp.dot(lhs[...], owbuf[...], preferred_element_type=f32).astype(bf16)
    finish(to_group(psum_buf, p_s, p_r))
    projected = psum_buf[0].astype(f32)
    for p in range(1, group):
        projected = projected + psum_buf[p].astype(f32)
    hidden = residual_ref[...].astype(f32) + projected
    hidden_ref[...] = hidden

    gained = (hidden * gain_ref[...].reshape(1, cols)).astype(bf16)
    picked = jnp.dot(sel16[...], gained, preferred_element_type=f32)
    for t in range(B):
        piece = picked[t * R : (t + 1) * R]
        disp_out[t] = jnp.concatenate([piece[:, :half], piece[:, half:]], axis=0).astype(bf16)
    dispatch = to_batch(lambda peer: disp_out.at[peer], disp_in.at[b], x_s, x_r)
    squares = jnp.sum(hidden * hidden, axis=1, keepdims=True)
    diag = lax.broadcasted_iota(jnp.int32, (tokens, 128), 0) == lax.broadcasted_iota(
        jnp.int32, (tokens, 128), 1
    )
    sq_row = jnp.sum(jnp.where(diag, squares, 0.0), axis=0, keepdims=True)
    sq_all[b] = jnp.broadcast_to(sq_row, (8, 128))
    sq_copies = to_batch(lambda peer: sq_all.at[b], sq_all.at[b], s_s, s_r)
    disp_in[b] = disp_out[b]
    z_row = 2 * lax.broadcasted_iota(jnp.int32, (128, 512), 0)
    z_col = lax.broadcasted_iota(jnp.int32, (128, 512), 1)
    place = jnp.where((z_col == z_row) | (z_col == z_row + 257), 1.0, 0.0).astype(bf16)
    finish(dispatch)

    @pl.loop(0, B)
    def _(s):
        got = disp_in[s].astype(f32)
        pieces = []
        for n in range(cols // 128):
            top_row = 0 if n * 128 < half else R
            at = n * 128 % half
            pieces.append(got[top_row : top_row + R, at : at + 128])
        spread_x = jnp.dot(
            jnp.concatenate(pieces, axis=0).astype(bf16), place, preferred_element_type=f32
        )
        for n in range(cols // 128):
            rows = spread_x[n * R : (n + 1) * R]
            to = pl.multiple_of(s * (2 * cols) + n * 256, 256)
            x2[:, pl.ds(to, 256)] = jnp.concatenate(
                [rows[:, :256], rows[:, 256:]], axis=0
            ).astype(bf16)

    finish(sq_copies)
    sq_total = sq_all[0]
    for t in range(1, B):
        sq_total = sq_total + sq_all[t]
    inverse = lax.rsqrt(sq_total / D + NORM_EPS)[0:1, 0:tokens]
    own = sel_ref[pl.ds(pl.multiple_of(b * R, 8), R), :]
    row_inverse = jnp.sum(own * inverse, axis=1, keepdims=True)
    row_number = lax.broadcasted_iota(jnp.int32, (R, ff), 0)

    back = []
    for e in range(pairs):
        res_ref[...] = jnp.zeros_like(res_ref)
        acc[...] = jnp.zeros_like(acc)

        @pl.loop(0, nchunk)
        def _(c):
            at = e * nchunk + c
            gate_copy(at).wait()
            weight = gbuf.at[at % NG].reshape(2 * CH, ff + 128)
            left = x2[:, pl.ds(pl.multiple_of(c * (2 * CH), 2 * CH), 2 * CH)]
            acc[...] += jnp.dot(left, weight[:, 0:ff], preferred_element_type=f32)

            @pl.when(at + NG < pairs * nchunk)
            def _():
                gate_copy(at + NG).start()

        gate = acc[0:R] * row_inverse
        up = acc[R : 2 * R] * row_inverse
        value = gate * (1.0 / (1.0 + jnp.exp(-gate))) * up
        held = (row_number >= e * CAPN) & (row_number < (e + 1) * CAPN)
        act_ref[...] = jnp.where(held, value, 0.0).astype(bf16)

        @pl.loop(0, ndown)
        def _(c):
            at = e * ndown + c
            down_copy(at).wait()
            left = act_ref[:, pl.ds(pl.multiple_of(c * DC, DC), DC)]
            res_ref[...] += jnp.dot(left, dbuf[at], preferred_element_type=f32)

        low = e * CAPN // 8 * 8
        for t in range(B):
            ret_out[e, t] = res_ref[low : low + BACK_ROWS, t * cols : (t + 1) * cols].astype(bf16)
        back = back + to_batch(
            lambda peer: ret_out.at[e, peer], ret_in.at[e, b], r_s, r_r, e * (B - 1)
        )
        ret_in[e, b] = ret_out[e, b]

    cb_ref[...] = jnp.zeros_like(cb_ref)
    finish(back)
    for e in range(pairs):
        low = e * CAPN // 8 * 8
        for t in range(B):
            cb_ref[t * R + low : t * R + low + BACK_ROWS] += ret_in[e, t].astype(f32)
    came = cb_ref[...].astype(bf16)
    combined = jnp.dot(whi_ref[...], came, preferred_element_type=f32) + jnp.dot(
        wlo_ref[...], came, preferred_element_type=f32
    )
    fin_buf[pos] = combined.astype(bf16)
    finish(to_group(fin_buf, f_s, f_r))
    mix = fin_buf[0].astype(f32)
    for p in range(1, group):
        mix = mix + fin_buf[p].astype(f32)
    out_ref[...] = (hidden_ref[...] + mix).astype(out_ref.dtype)


def fused(
    queries, newest, cache, lengths, page_ids, out_weight, residual, gain, ids, route, gate_up, down
):
    S, B, H = lax.axis_size("sect"), lax.axis_size("batch"), lax.axis_size("head")
    seqs, qh, _ = queries.shape
    hd = newest.shape[2] // 2
    tokens, cols = residual.shape
    pairs, depth, _, ff = gate_up.shape
    capn = 2 * tokens * ids.shape[1] // EXPERTS
    R = pairs * capn
    CH, DC = 512, 256
    keys = cache.shape[1] * cache.shape[2]
    slots = B * R
    group = S * H
    bf16, f32 = jnp.bfloat16, jnp.float32
    V, dma = pltpu.VMEM, pltpu.SemaphoreType.DMA
    vm, hbm = pl.BlockSpec(memory_space=pltpu.VMEM), pl.BlockSpec(memory_space=pl.ANY)
    smem = pl.BlockSpec(memory_space=pltpu.SMEM)
    ndown = ff // DC
    return pl.pallas_call(
        functools.partial(layer_kernel, (S, B, H, R, capn, CH, DC)),
        out_shape=jax.ShapeDtypeStruct((tokens, cols), bf16),
        in_specs=[vm, vm, smem, vm, vm, vm, vm, vm, hbm, hbm, hbm, hbm],
        out_specs=vm,
        scratch_shapes=[
            V((CACHE_SLOTS,) + cache.shape[1:], bf16), V(out_weight.shape, bf16),
            V((NG, CH, 2, ff + 128), bf16),
            V((pairs * ndown, DC, depth), bf16),
            V((-(-seqs // 8) * 8, keys), f32), V((seqs, qh, hd), f32), V((H, seqs, qh, hd), f32),
            V((B, seqs, qh * H, hd), bf16), V((tokens, qh * H, hd), f32),
            V((tokens, qh * H * hd), bf16), V((group, tokens, cols), bf16), V((tokens, cols), f32),
            V((B, 8, 128), f32),
            V((slots, tokens), f32), V((slots, tokens), bf16), V((tokens, slots), bf16),
            V((tokens, slots), bf16), V((B, 2 * R, cols // 2), bf16),
            V((B, 2 * R, cols // 2), bf16), V((2 * R, 2 * depth), bf16), V((2 * R, ff), f32),
            V((R, ff), bf16), V((R, depth), f32),
            V((pairs, B, BACK_ROWS, cols), bf16), V((pairs, B, BACK_ROWS, cols), bf16),
            V((slots, cols), f32),
            V((group, tokens, cols), bf16),
            dma((CACHE_SLOTS,)), dma, dma((NG,)), dma((pairs * ndown,)), dma((2,)),
            dma((2 * (B - 1),)), dma((2 * (B - 1),)), dma((group - 1,)), dma((group - 1,)),
            dma((B - 1,)), dma((B - 1,)), dma((B - 1,)), dma((B - 1,)),
            dma((pairs * (B - 1),)), dma((pairs * (B - 1),)), dma((group - 1,)), dma((group - 1,)),
        ],
        compiler_params=pltpu.CompilerParams(
            collective_id=0, has_side_effects=True, vmem_limit_bytes=63 * 1024 * 1024
        ),
        cost_estimate=pl.CostEstimate(
            flops=4 * R * depth * ff * pairs * 3,
            bytes_accessed=2 * (gate_up.size + down.size + cache.size), transcendentals=0,
        ),
    )(queries, newest, lengths, page_ids, residual, gain, ids.T, route.T,
      cache, out_weight, gate_up, down)


def solution(mesh):
    placed = (
        P("batch", "head", "sect"),
        P("batch", None, None),
        P("batch", ("sect", "head"), None, None),
        P("batch"),
        P("batch", None, None),
        P(("sect", "head"), "batch"),
        P(None, "batch"),
        P("batch"),
        P(),
        P(),
        P(("sect", "batch"), None, None, "head"),
        P(("sect", "batch"), "head", None),
    )
    whole_parts = mesh.shape["sect"] * mesh.shape["head"] == 4 and mesh.shape["head"] == 2
    body = fused if whole_parts else on_device
    return jax.shard_map(
        body, mesh=mesh, in_specs=placed, out_specs=P(None, "batch"), check_vma=False
    )
```
